256 devices in a mesh: row: 4 (over y), col: 16 (over x, z_lo, core), depth: 4 (over z_hi).
Axes of the slice: x: 4, y: 4, z: 8 (z_hi: 4, z_lo: 2; z = z_hi * 2 + z_lo), core: 2. Of those that a mesh axis runs over, the one named last changes fastest.
Arguments:
- left_pair: bfloat16 [512, 4, 512, 128], P('row', 'depth', 'col'), may hold values from -6 to 6
- right_pair: bfloat16 [832, 4, 512, 128], P('col', 'depth', 'row'), may hold values from -6 to 6
- pair_tile: bfloat16 [512, 832, 128], P('row', ('col', 'depth')), may hold values from -6 to 6
- row_flags: int32 [512], P('row'), may hold values 0 or 1
- column_flags: int32 [832], P('col'), may hold values 0 or 1
- key_flags: int32 [4, 512], replicated, may hold values 0 or 1
- input_gain: float32 [128], replicated, may hold values from 0.5 to 1.5
- input_bias: float32 [128], replicated, may hold values from -1.75 to 1.75
- left_gate_weight: bfloat16 [128, 128], replicated, may hold values from -0.5 to 0.5
- left_value_weight: bfloat16 [128, 128], replicated, may hold values from -0.5 to 0.5
- right_gate_weight: bfloat16 [128, 128], replicated, may hold values from -0.5 to 0.5
- right_value_weight: bfloat16 [128, 128], replicated, may hold values from -0.5 to 0.5
- hidden_gain: float32 [128], replicated, may hold values from 0.5 to 1.5
- hidden_bias: float32 [128], replicated, may hold values from -1.75 to 1.75
- output_gate_weight: bfloat16 [128, 128], replicated, may hold values from -0.5 to 0.5
- output_weight: bfloat16 [128, 128], replicated, may hold values from -0.5 to 0.5
Outputs:
- update: bfloat16 [512, 832, 128], P('row', ('col', 'depth'))
The draws below stay inside these ranges and needn't reach their ends.
All inputs are finite; a program needn't handle non-finite values. No bound on the sum of `row_flags` or of `column_flags` on one device may be relied on, other than what follows from the above.
Results may differ from the reference program's by a relative error of at most 0.0055.
Values may be sent and summed in bfloat16 or wider, within the bound.
A program may use at most 128 MiB of HBM per device.

```python
import jax
import jax.numpy as jnp
from jax import lax

CZ = 128
CH = 128
QUARTER = 512
ROWS = 512
COLS = 832
KEYS = 2048
N_DEPTH = 4


def touch_ends(drawn, stream_key, least, largest):
    dims = drawn.shape
    place = [jax.random.randint(jax.random.fold_in(stream_key, axis), (), 0, dims[axis]) for axis in range(len(dims))]
    drawn = drawn.at[tuple(place)].set(least)
    longest = dims.index(max(dims))
    place[longest] = (place[longest] + 1) % dims[longest]
    return drawn.at[tuple(place)].set(largest)


def block_levels(key, shape, cuts, low, high):
    level, own = 1.0, jax.random.fold_in(key, 6)
    for axis_at, blocks in cuts:
        draws = jnp.exp(jax.random.uniform(jax.random.fold_in(own, axis_at), (blocks,), jnp.float32, low / len(cuts), high / len(cuts)))
        level = level * jnp.repeat(draws, shape[axis_at] // blocks).reshape([-1 if axis == axis_at else 1 for axis in range(len(shape))])
    return level


def bell_draw(rng, shape, scale, limit, cuts=(), kind=jnp.bfloat16):
    result = scale * jax.random.normal(rng, shape, jnp.float32)
    if cuts:
        result = result * block_levels(rng, shape, cuts, -0.22, 0.18)
    return jnp.clip(result, -limit, limit).astype(kind)


def setup_inputs(seed: int = 0) -> dict:
    seeds = jax.random.split(jax.random.key(seed), 17)
    left_pair = bell_draw(seeds[0], (ROWS, N_DEPTH, QUARTER, CZ), 1.0, 6.0, ((0, 4), (1, 4), (2, 16)))
    right_pair = bell_draw(seeds[1], (COLS, N_DEPTH, QUARTER, CZ), 1.0, 6.0, ((0, 16), (1, 4), (2, 4)))
    pair_tile = bell_draw(seeds[2], (ROWS, COLS, CZ), 1.0, 6.0, ((0, 4), (1, 64)))
    row_flags = touch_ends((jax.random.randint(seeds[3], (ROWS,), 0, 8) < 7).astype(jnp.int32), jax.random.fold_in(seeds[3], 1), 0, 1)
    column_flags = touch_ends((jax.random.randint(seeds[4], (COLS,), 0, 8) < 7).astype(jnp.int32), jax.random.fold_in(seeds[4], 1), 0, 1)
    key_flags = touch_ends((jax.random.randint(seeds[5], (N_DEPTH, QUARTER), 0, 8) < 7).astype(jnp.int32), jax.random.fold_in(seeds[5], 1), 0, 1)
    input_gain = jnp.clip(1.0 + 0.1 * jax.random.normal(seeds[6], (CZ,), jnp.float32), 0.5, 1.5)
    input_bias = bell_draw(seeds[7], (CZ,), 0.3, 1.75, (), jnp.float32)
    left_gate_weight = bell_draw(seeds[8], (CZ, CH), CZ ** -0.5, 0.5)
    left_value_weight = bell_draw(seeds[9], (CZ, CH), CZ ** -0.5, 0.5)
    right_gate_weight = bell_draw(seeds[10], (CZ, CH), CZ ** -0.5, 0.5)
    right_value_weight = bell_draw(seeds[11], (CZ, CH), CZ ** -0.5, 0.5)
    hidden_gain = jnp.clip(1.0 + 0.1 * jax.random.normal(seeds[12], (CH,), jnp.float32), 0.5, 1.5)
    hidden_bias = bell_draw(seeds[13], (CH,), 0.3, 1.75, (), jnp.float32)
    output_gate_weight = bell_draw(seeds[14], (CZ, CZ), CZ ** -0.5, 0.5)
    output_weight = bell_draw(seeds[15], (CH, CZ), CH ** -0.5, 0.5)
    return {"left_pair": left_pair, "right_pair": right_pair, "pair_tile": pair_tile, "row_flags": row_flags, "column_flags": column_flags, "key_flags": key_flags, "input_gain": input_gain, "input_bias": input_bias, "left_gate_weight": left_gate_weight, "left_value_weight": left_value_weight, "right_gate_weight": right_gate_weight, "right_value_weight": right_value_weight, "hidden_gain": hidden_gain, "hidden_bias": hidden_bias, "output_gate_weight": output_gate_weight, "output_weight": output_weight}


EPSILON = 1e-05

def layer_norm(values, norm_gain, norm_bias):
    widened = values.astype(jnp.float32)
    centre = lax.optimization_barrier(jnp.mean(widened, axis=-1, keepdims=True))
    shifted = widened - centre
    spread = lax.optimization_barrier(jnp.mean(shifted * shifted, axis=-1, keepdims=True))
    scaled = shifted * lax.rsqrt(spread + EPSILON) * norm_gain.astype(jnp.float32) + norm_bias.astype(jnp.float32)
    return scaled.astype(jnp.bfloat16)

def gated_values(pair, input_gain, input_bias, gate_weight, value_weight, mask):
    normed = layer_norm(pair, input_gain, input_bias)
    gating = jax.nn.sigmoid(jnp.dot(normed, gate_weight, preferred_element_type=jnp.float32))
    content = jnp.dot(normed, value_weight, preferred_element_type=jnp.float32)
    return (mask[..., None] * gating * content).astype(jnp.bfloat16)

def reference(left_pair, right_pair, pair_tile, row_flags, column_flags, key_flags, input_gain, input_bias, left_gate_weight, left_value_weight, right_gate_weight, right_value_weight, hidden_gain, hidden_bias, output_gate_weight, output_weight):
    row_mask = row_flags.astype(jnp.float32)
    column_mask = column_flags.astype(jnp.float32)
    key_mask = key_flags.astype(jnp.float32)
    left_mask = row_mask[:, None, None] * key_mask[None, :, :]
    left_act = gated_values(left_pair, input_gain, input_bias, left_gate_weight, left_value_weight, left_mask)

    def right_quarter(inputs):
        pair_quarter, keys_quarter = inputs
        quarter_mask = column_mask[:, None] * keys_quarter[None, :]
        return gated_values(pair_quarter, input_gain, input_bias, right_gate_weight, right_value_weight, quarter_mask)
    right_act = lax.map(right_quarter, (jnp.moveaxis(right_pair, 1, 0), key_mask))
    left_flat = left_act.reshape(ROWS, KEYS, CH)
    right_flat = jnp.moveaxis(right_act, 0, 1).reshape(COLS, KEYS, CH)
    width = 16 if CH % 16 == 0 else CH
    count = CH // width
    left_blocks = jnp.moveaxis(left_flat.reshape(ROWS, KEYS, count, width), 2, 0)
    right_blocks = jnp.moveaxis(right_flat.reshape(COLS, KEYS, count, width), 2, 0)

    def contract(inputs):
        left_block, right_block = inputs
        return jnp.einsum('ikh,jkh->ijh', left_block.astype(jnp.float32), right_block.astype(jnp.float32), precision=lax.Precision.HIGHEST)
    combined = jnp.moveaxis(lax.map(contract, (left_blocks, right_blocks)), 0, 2).reshape(ROWS, COLS, CH)
    hidden_normed = layer_norm(combined, hidden_gain, hidden_bias)
    tile_normed = layer_norm(pair_tile, input_gain, input_bias)
    gating = jax.nn.sigmoid(jnp.dot(tile_normed, output_gate_weight, preferred_element_type=jnp.float32))
    projected = jnp.dot(hidden_normed, output_weight, preferred_element_type=jnp.float32)
    return (gating * projected).astype(jnp.bfloat16)
```

```python
import functools

import jax
import jax.numpy as jnp
from jax import lax
from jax.experimental import pallas as pl
from jax.experimental.pallas import tpu as pltpu
from jax.sharding import PartitionSpec as P

EPSILON = 1e-05
MESH = pl.DeviceIdType.MESH
F32 = jnp.float32
BF16 = jnp.bfloat16

NI, NM, NJ, NK, NT = 128, 32, 52, 128, 13
HB = 8
JPAD = NT + 1
MSG = JPAD * HB
SLOTS = 80
BASE = 16

ROUND = (2, 1, 3, 0)
NEAR = [(dx, dy) for dx in ROUND for dy in ROUND]


def normalise(values):
    centre = jnp.mean(values, axis=-1, keepdims=True)
    shifted = values - centre
    spread = jnp.mean(shifted * shifted, axis=-1, keepdims=True)
    return shifted * lax.rsqrt(spread + EPSILON)


def sigmoid(values):
    return 0.5 * jnp.tanh(0.5 * values) + 0.5


def dot_nt(left, right):
    return lax.dot_general(left, right, (((1,), (1,)), ((), ())), preferred_element_type=F32)


def kernel(
    xl, xr, xt, row_flags, column_flags, key_scalars, key_rows,
    gain, bias, wlg, wlv, wrg, wrv, hgain, hbias, wog, wo,
    out,
    nl, tl, tr, ls, lb, rs, rb, osc, os_, cb, gate, fin,
    sl, rl, sr, rr, sf, rf, so, ro, cs,
):
    row = lax.axis_index("row")
    col = lax.axis_index("col")
    depth = lax.axis_index("depth")
    x = lax.div(col, 4)
    low = lax.rem(col, 4)
    core_mate = x * 4 + low + 1 - 2 * lax.rem(low, 2)
    mate_low = lax.rem(low + 2, 4)
    z_mate = x * 4 + mate_low
    other_low = low + 1 - 2 * lax.rem(low, 2)

    def at(dx, dy, dz=0):
        return (
            lax.rem(row + dy, 4),
            lax.rem(x + dx, 4) * 4 + low,
            lax.rem(depth + dz, 4),
        )

    barrier = pltpu.get_barrier_semaphore()
    peers = [at(dx, dy, dz) for dz in range(4) for dx, dy in NEAR if (dx, dy, dz) != (0, 0, 0)]
    peers += [(row, core_mate, depth), (row, z_mate, depth)]
    for peer in peers:
        pl.semaphore_signal(barrier, inc=1, device_id=peer, device_id_type=MESH)

    gains, biases = gain[...], bias[...]

    def left_norm(step, carry):
        rows = pl.ds(pl.multiple_of(step * 256, 256), 256)
        nl[rows, :] = normalise(xl[rows, :].astype(F32)) * gains + biases
        return carry

    lax.fori_loop(0, NI * NM // 256, left_norm, 0)
    w_left = jnp.concatenate([wlg[...], wlv[...]], axis=1).astype(F32).T.astype(BF16)
    row_mask = row_flags[...].astype(F32)

    def left_act(step, carry):
        xs = jnp.concatenate(
            [nl[pl.ds(step * 4 + mm, NI, stride=NM), :] for mm in range(4)], axis=0
        ).astype(BF16)
        both = dot_nt(w_left, xs)
        act = sigmoid(both[:128]) * both[128:]
        for mm in range(4):
            key = key_scalars[depth, col * NM + step * 4 + mm].astype(F32)
            part = act[:, mm * NI : (mm + 1) * NI] * (row_mask * key)
            for d in range(16):
                tl[pl.ds(d * HB * NM + step * 4 + mm, HB, stride=NM), :] = part[d * HB : (d + 1) * HB]
        return carry

    lax.fori_loop(0, NM // 4, left_act, 0)

    pl.semaphore_wait(barrier, len(peers))

    def owner(dx, dy):
        return lax.rem(x + dx, 4) * 4 + lax.rem(row + dy, 4)

    left_sends = {}
    for n, (dx, dy) in enumerate(NEAR):
        d = owner(dx, dy)
        rows = pl.ds(pl.multiple_of(d * HB * NM, HB * NM), HB * NM)
        ls[d] = tl[rows, :].astype(BF16).reshape(HB, NM, NI)
        target = lb.at[row, :, x, low]
        if (dx, dy) == (0, 0):
            pltpu.make_async_copy(ls.at[d], target, cs.at[0]).start()
            continue
        copy = pltpu.make_async_remote_copy(
            src_ref=ls.at[d], dst_ref=target, send_sem=sl.at[n], recv_sem=rl.at[n],
            device_id=at(dx, dy), device_id_type=MESH,
        )
        copy.start()
        left_sends[dx, dy] = copy

    w_right = jnp.concatenate([wrg[...], wrv[...]], axis=1).astype(F32).T.astype(BF16)
    key_block = key_rows[:, pl.ds(pl.multiple_of(row * NK, NK), NK)].astype(F32)
    here = lax.broadcasted_iota(jnp.int32, (4, NK), 0) == depth
    key_mask = jnp.sum(jnp.where(here, key_block, 0.0), axis=0, keepdims=True)

    def right_act(step, carry):
        rows = pl.ds(pl.multiple_of(step * 512, 512), 512)
        xs = (normalise(xr[rows, :].astype(F32)) * gains + biases).astype(BF16)
        both = dot_nt(w_right, xs)
        act = sigmoid(both[:128]) * both[128:]
        for jj in range(4):
            flag = column_flags[step * 4 + jj].astype(F32)
            part = act[:, jj * NK : (jj + 1) * NK] * (key_mask * flag)
            for d in range(16):
                tr[pl.ds(d * HB * NJ + step * 4 + jj, HB, stride=NJ), :] = part[d * HB : (d + 1) * HB]
        return carry

    lax.fori_loop(0, NJ // 4, right_act, 0)

    right_sends = {}
    for n, (dx, dy) in enumerate(NEAR):
        d = owner(dx, dy)
        rows = pl.ds(pl.multiple_of(d * HB * NJ, HB * NJ), HB * NJ)
        if (dx, dy) == (0, 0):
            rb[x, row] = tr[rows, :].astype(BF16)
            continue
        rs[d] = tr[rows, :].astype(BF16)
        copy = pltpu.make_async_remote_copy(
            src_ref=rs.at[d], dst_ref=rb.at[x, row], send_sem=sr.at[n], recv_sem=rr.at[n],
            device_id=at(dx, dy), device_id_type=MESH,
        )
        copy.start()
        right_sends[dx, dy] = copy

    def received(n, dst, sem):
        pltpu.make_async_remote_copy(
            src_ref=dst, dst_ref=dst, send_sem=sem, recv_sem=sem,
            device_id=at(1, 0), device_id_type=MESH,
        ).wait_recv()

    def source(dx, dy):
        return lax.rem(x + 4 - dx, 4), lax.rem(row + 4 - dy, 4)

    forwards = []

    def forward(n, y_from, share, device):
        part = lb.at[y_from, :, :, share]
        copy = pltpu.make_async_remote_copy(
            src_ref=part, dst_ref=part, send_sem=sf.at[n], recv_sem=rf.at[n],
            device_id=device, device_id_type=MESH,
        )
        copy.start()
        forwards.append(copy)

    pltpu.make_async_copy(ls.at[owner(0, 0)], lb.at[row, :, x, low], cs.at[0]).wait()
    for g, dy in enumerate(ROUND):
        for dx in ROUND:
            if (dx, dy) != (0, 0):
                x_from, y_from = source(dx, dy)
                n = NEAR.index((dx, dy))
                received(n, lb.at[y_from, :, x_from, low], rl.at[n])
        y_from = lax.rem(row + 4 - dy, 4)
        forward(g, y_from, low, (row, z_mate, depth))
        forward(4 + g, y_from, low, (row, core_mate, depth))

    tile_weight = wog[...]

    def tile_gate(step, carry):
        rows = pl.ds(step * 16, 16)
        padded = jnp.concatenate(
            [xt[rows].astype(F32), jnp.zeros((16, 16 - NT, 128), F32)], axis=1
        ).reshape(256, 128)
        normed = (normalise(padded) * gains + biases).astype(BF16)
        logits = jnp.dot(normed, tile_weight, preferred_element_type=F32)
        gate[pl.ds(pl.multiple_of(step * 256, 256), 256), :] = sigmoid(logits)
        return carry

    lax.fori_loop(0, NI // 16, tile_gate, 0)

    for g, dy in enumerate(ROUND):
        y_from = lax.rem(row + 4 - dy, 4)
        received(g, lb.at[y_from, :, :, mate_low], rf.at[g])
        forward(8 + g, y_from, mate_low, (row, core_mate, depth))
    mate_other = lax.rem(other_low + 2, 4)
    for g, dy in enumerate(ROUND):
        y_from = lax.rem(row + 4 - dy, 4)
        received(4 + g, lb.at[y_from, :, :, other_low], rf.at[4 + g])
        received(8 + g, lb.at[y_from, :, :, mate_other], rf.at[8 + g])

    osc[:, (BASE + NJ) * HB : (BASE + NJ + 1) * HB, :] = jnp.zeros((4, HB, 128), F32)
    out_sends = []
    count = 0
    mine = x * 4 + row
    for stage, dx in enumerate(ROUND):
        x_from = lax.rem(x + 4 - dx, 4)
        for dy in ROUND:
            if (dx, dy) != (0, 0):
                y_from = lax.rem(row + 4 - dy, 4)
                n = NEAR.index((dx, dy))
                received(n, rb.at[x_from, y_from], rr.at[n])
        for h in range(HB):
            first = h * NJ // 16 * 16
            skew = h * NJ - first
            lhs = jnp.concatenate([rb[x_from, y, first : first + 64, :] for y in range(4)], axis=1)
            for half in range(2):
                rhs = jnp.concatenate(
                    [lb[half * 2 + q, h].reshape(512, NI) for q in range(2)], axis=1
                )
                sums = jnp.dot(lhs, rhs, preferred_element_type=F32)
                for q in range(2):
                    osc[half * 2 + q, pl.ds((BASE - skew) * HB + h, 64, stride=HB), :] = sums[
                        :, q * NI : (q + 1) * NI
                    ]
        for dz in (2, 1, 3, 0):
            to_depth = lax.rem(depth + dz, 4)
            for dy in ROUND:
                to_row = lax.rem(row + dy, 4)
                start = pl.multiple_of(BASE * HB + to_depth * (NT * HB), HB)
                block = osc[to_row, pl.ds(start, MSG), :].astype(BF16)
                target = cb.at[depth, mine]
                if (dx, dy, dz) == (0, 0, 0):
                    cb[depth, mine] = block
                    continue
                os_[stage, to_row, to_depth] = block
                copy = pltpu.make_async_remote_copy(
                    src_ref=os_.at[stage, to_row, to_depth], dst_ref=target,
                    send_sem=so.at[count], recv_sem=ro.at[count],
                    device_id=(to_row, x_from * 4 + low, to_depth), device_id_type=MESH,
                )
                copy.start()
                out_sends.append((dx, dy, dz, count, copy))
                count += 1

    for dx, dy, dz, n, copy in out_sends:
        x_at = lax.rem(x + dx, 4)
        y_at = lax.rem(row + 4 - dy, 4)
        d_at = lax.rem(depth + 4 - dz, 4)
        received(n, cb.at[d_at, x_at * 4 + y_at], ro.at[n])

    hg = jnp.broadcast_to(hgain[...], (128, 128)).T
    hb = jnp.broadcast_to(hbias[...], (128, 128)).T
    weight = wo[...]

    def finish(j, sums):
        centre = jnp.mean(sums, axis=0, keepdims=True)
        shifted = sums - centre
        spread = jnp.mean(shifted * shifted, axis=0, keepdims=True)
        hidden = (shifted * lax.rsqrt(spread + EPSILON) * hg + hb).astype(BF16)
        projected = lax.dot_general(
            hidden, weight, (((0,), (0,)), ((), ())), preferred_element_type=F32
        )
        fin[pl.ds(j, NI, stride=16), :] = projected

    def pair_of_columns(p, carry):
        rows = pl.ds(pl.multiple_of(p * 16, 16), 16)
        total = cb[0, :, rows, :].astype(F32)
        for z in range(1, 4):
            total = total + cb[z, :, rows, :].astype(F32)
        finish(p * 2, total[:, :HB].reshape(128, NI))
        finish(p * 2 + 1, total[:, HB:].reshape(128, NI))
        return carry

    lax.fori_loop(0, JPAD // 2, pair_of_columns, 0)

    def write(step, carry):
        rows = pl.ds(pl.multiple_of(step * 256, 256), 256)
        result = (gate[rows, :] * fin[rows, :]).reshape(16, 16, 128)
        out[pl.ds(step * 16, 16)] = result[:, :NT, :].astype(BF16)
        return carry

    lax.fori_loop(0, NI // 16, write, 0)

    for copy in list(left_sends.values()) + list(right_sends.values()) + forwards:
        copy.wait_send()
    for item in out_sends:
        item[4].wait_send()


def per_device(
    left_pair, right_pair, pair_tile, row_flags, column_flags, key_flags,
    input_gain, input_bias, left_gate_weight, left_value_weight,
    right_gate_weight, right_value_weight, hidden_gain, hidden_bias,
    output_gate_weight, output_weight,
):
    vmem = pl.BlockSpec(memory_space=pltpu.VMEM)
    smem = pl.BlockSpec(memory_space=pltpu.SMEM)
    dma = pltpu.SemaphoreType.DMA
    return pl.pallas_call(
        kernel,
        out_shape=jax.ShapeDtypeStruct((NI, NT, 128), BF16),
        in_specs=[vmem] * 4 + [smem] * 2 + [vmem] * 11,
        out_specs=vmem,
        scratch_shapes=[
            pltpu.VMEM((NI * NM, 128), F32),
            pltpu.VMEM((16 * HB * NM, 128), F32),
            pltpu.VMEM((16 * HB * NJ, 128), F32),
            pltpu.VMEM((16, HB, NM, NI), BF16),
            pltpu.VMEM((4, HB, 4, 4, NM, NI), BF16),
            pltpu.VMEM((16, HB * NJ, NK), BF16),
            pltpu.VMEM((4, 4, HB * NJ, NK), BF16),
            pltpu.VMEM((4, SLOTS * HB, 128), F32),
            pltpu.VMEM((4, 4, 4, MSG, 128), BF16),
            pltpu.VMEM((4, 16, MSG, 128), BF16),
            pltpu.VMEM((NI * 16, 128), F32),
            pltpu.VMEM((NI * 16, 128), F32),
            dma((16,)), dma((16,)), dma((16,)), dma((16,)),
            dma((12,)), dma((12,)), dma((63,)), dma((63,)), dma((1,)),
        ],
        compiler_params=pltpu.CompilerParams(
            collective_id=0, has_side_effects=True, vmem_limit_bytes=48 * 2**20
        ),
        name="triangle",
    )(
        left_pair.reshape(NI * NM, 128),
        right_pair.reshape(NJ * NK, 128),
        pair_tile,
        row_flags.reshape(1, NI),
        column_flags,
        key_flags,
        key_flags,
        input_gain.reshape(1, 128),
        input_bias.reshape(1, 128),
        left_gate_weight, left_value_weight, right_gate_weight, right_value_weight,
        hidden_gain.reshape(1, 128),
        hidden_bias.reshape(1, 128),
        output_gate_weight, output_weight,
    )


def solution(mesh):
    in_specs = (
        P("row", "depth", "col", None),
        P("col", "depth", "row", None),
        P("row", ("col", "depth"), None),
        P("row"),
        P("col"),
    ) + (P(),) * 11
    return jax.shard_map(
        per_device,
        mesh=mesh,
        in_specs=in_specs,
        out_specs=P("row", ("col", "depth"), None),
        check_vma=False,
    )
```

```python
import functools

import jax
import jax.numpy as jnp
from jax import lax
from jax.experimental import pallas as pl
from jax.experimental.pallas import tpu as pltpu
from jax.sharding import PartitionSpec as P

EPSILON = 1e-05
MESH = pl.DeviceIdType.MESH
F32 = jnp.float32
BF16 = jnp.bfloat16

NI, NM, NJ, NK, NT = 128, 32, 52, 128, 13
HB = 8
JPAD = NT + 1
MSG = JPAD * HB
SLOTS = 80
BASE = 16

ROUND = (2, 1, 3, 0)
VIA = ((2, 0), (1, 3))
NEAR = [(dx, dy) for dx in ROUND for dy in ROUND]


LOAD_ORDER = (0, 7, 8, 9, 10, 3, 5, 1, 11, 12, 4, 6, 2, 15, 13, 14, 16)


def normalise(values):
    centre = jnp.mean(values, axis=-1, keepdims=True)
    shifted = values - centre
    spread = jnp.mean(shifted * shifted, axis=-1, keepdims=True)
    return shifted * lax.rsqrt(spread + EPSILON)


def sigmoid(values):
    return 0.5 * jnp.tanh(0.5 * values) + 0.5


def dot_nt(left, right):
    return lax.dot_general(left, right, (((1,), (1,)), ((), ())), preferred_element_type=F32)


def kernel(*refs):
    sources, refs = refs[:17], refs[17:]
    out, refs = refs[0], refs[1:]
    held, refs = refs[:17], refs[17:]
    (
        xl, xr, xt, row_flags, column_flags, key_scalars, key_rows,
        gain, bias, wlg, wlv, wrg, wrv, hgain, hbias, wog, wo,
    ) = held
    (
        nl, tl, tr, ls, lb, rs, rb, osc, av, ar, os_, cb, gate,
        sl, rl, sr, rr, sf, rf, sa, ra, so, ro, cs, loads,
    ) = refs
    pending = [
        pltpu.make_async_copy(src, dst, loads.at[n])
        for n, (src, dst) in enumerate(zip(sources, held))
    ]
    for n in LOAD_ORDER:
        pending[n].start()

    def loaded(*numbers):
        for n in numbers:
            pending[n].wait()

    row = lax.axis_index("row")
    col = lax.axis_index("col")
    depth = lax.axis_index("depth")
    x = lax.div(col, 4)
    low = lax.rem(col, 4)
    core_mate = x * 4 + low + 1 - 2 * lax.rem(low, 2)
    mate_low = lax.rem(low + 2, 4)
    z_mate = x * 4 + mate_low
    other_low = low + 1 - 2 * lax.rem(low, 2)

    def at(dx, dy, dz=0):
        return (
            lax.rem(row + dy, 4),
            lax.rem(x + dx, 4) * 4 + low,
            lax.rem(depth + dz, 4),
        )

    barrier = pltpu.get_barrier_semaphore()
    peers = [at(dx, dy, dz) for dz in (0, 1, 3) for dx, dy in NEAR if (dx, dy, dz) != (0, 0, 0)]
    peers += [(row, core_mate, depth), (row, z_mate, depth)]
    for peer in peers:
        pl.semaphore_signal(barrier, inc=1, device_id=peer, device_id_type=MESH)

    loaded(0, 7, 8, 9, 10, 3, 5)
    gains, biases = gain[...], bias[...]

    def left_norm(step, carry):
        rows = pl.ds(pl.multiple_of(step * 256, 256), 256)
        nl[rows, :] = normalise(xl[rows, :].astype(F32)) * gains + biases
        return carry

    lax.fori_loop(0, NI * NM // 256, left_norm, 0)
    w_left = jnp.concatenate([wlg[...], wlv[...]], axis=1).astype(F32).T.astype(BF16)
    row_mask = row_flags[...].astype(F32)

    def left_act(step, carry):
        xs = jnp.concatenate(
            [nl[pl.ds(step * 4 + mm, NI, stride=NM), :] for mm in range(4)], axis=0
        ).astype(BF16)
        both = dot_nt(w_left, xs)
        act = sigmoid(both[:128]) * both[128:]
        for mm in range(4):
            key = key_scalars[depth, col * NM + step * 4 + mm].astype(F32)
            part = act[:, mm * NI : (mm + 1) * NI] * (row_mask * key)
            for d in range(16):
                tl[pl.ds(d * HB * NM + step * 4 + mm, HB, stride=NM), :] = part[d * HB : (d + 1) * HB]
        return carry

    lax.fori_loop(0, NM // 4, left_act, 0)

    pl.semaphore_wait(barrier, len(peers))

    def owner(dx, dy):
        return lax.rem(x + dx, 4) * 4 + lax.rem(row + dy, 4)

    left_sends = {}
    for n, (dx, dy) in enumerate(NEAR):
        d = owner(dx, dy)
        rows = pl.ds(pl.multiple_of(d * HB * NM, HB * NM), HB * NM)
        ls[d] = tl[rows, :].astype(BF16).reshape(HB, NM, NI)
        target = lb.at[row, :, x, low]
        if (dx, dy) == (0, 0):
            pltpu.make_async_copy(ls.at[d], target, cs.at[0]).start()
            continue
        copy = pltpu.make_async_remote_copy(
            src_ref=ls.at[d], dst_ref=target, send_sem=sl.at[n], recv_sem=rl.at[n],
            device_id=at(dx, dy), device_id_type=MESH,
        )
        copy.start()
        left_sends[dx, dy] = copy

    loaded(1, 11, 12, 4, 6)
    w_right = jnp.concatenate([wrg[...], wrv[...]], axis=1).astype(F32).T.astype(BF16)
    key_block = key_rows[:, pl.ds(pl.multiple_of(row * NK, NK), NK)].astype(F32)
    here = lax.broadcasted_iota(jnp.int32, (4, NK), 0) == depth
    key_mask = jnp.sum(jnp.where(here, key_block, 0.0), axis=0, keepdims=True)

    def right_act(step, carry):
        rows = pl.ds(pl.multiple_of(step * 512, 512), 512)
        xs = (normalise(xr[rows, :].astype(F32)) * gains + biases).astype(BF16)
        both = dot_nt(w_right, xs)
        act = sigmoid(both[:128]) * both[128:]
        for jj in range(4):
            flag = column_flags[step * 4 + jj].astype(F32)
            part = act[:, jj * NK : (jj + 1) * NK] * (key_mask * flag)
            for d in range(16):
                tr[pl.ds(d * HB * NJ + step * 4 + jj, HB, stride=NJ), :] = part[d * HB : (d + 1) * HB]
        return carry

    lax.fori_loop(0, NJ // 4, right_act, 0)

    right_sends = {}
    for n, (dx, dy) in enumerate(NEAR):
        d = owner(dx, dy)
        rows = pl.ds(pl.multiple_of(d * HB * NJ, HB * NJ), HB * NJ)
        if (dx, dy) == (0, 0):
            rb[x, row] = tr[rows, :].astype(BF16)
            continue
        rs[d] = tr[rows, :].astype(BF16)
        copy = pltpu.make_async_remote_copy(
            src_ref=rs.at[d], dst_ref=rb.at[x, row], send_sem=sr.at[n], recv_sem=rr.at[n],
            device_id=at(dx, dy), device_id_type=MESH,
        )
        copy.start()
        right_sends[dx, dy] = copy

    def received(n, dst, sem):
        pltpu.make_async_remote_copy(
            src_ref=dst, dst_ref=dst, send_sem=sem, recv_sem=sem,
            device_id=at(1, 0), device_id_type=MESH,
        ).wait_recv()

    def source(dx, dy):
        return lax.rem(x + 4 - dx, 4), lax.rem(row + 4 - dy, 4)

    forwards = []

    def forward(n, y_from, share, device):
        part = lb.at[y_from, :, :, share]
        copy = pltpu.make_async_remote_copy(
            src_ref=part, dst_ref=part, send_sem=sf.at[n], recv_sem=rf.at[n],
            device_id=device, device_id_type=MESH,
        )
        copy.start()
        forwards.append(copy)

    pltpu.make_async_copy(ls.at[owner(0, 0)], lb.at[row, :, x, low], cs.at[0]).wait()
    for g, dy in enumerate(ROUND):
        for dx in ROUND:
            if (dx, dy) != (0, 0):
                x_from, y_from = source(dx, dy)
                n = NEAR.index((dx, dy))
                received(n, lb.at[y_from, :, x_from, low], rl.at[n])
        y_from = lax.rem(row + 4 - dy, 4)
        forward(g, y_from, low, (row, z_mate, depth))
        forward(4 + g, y_from, low, (row, core_mate, depth))

    loaded(2, 15, 13, 14, 16)
    tile_weight = wog[...]

    def tile_gate(j, carry):
        normed = (normalise(xt[j].astype(F32)) * gains + biases).astype(BF16)
        gate[j] = sigmoid(jnp.dot(normed, tile_weight, preferred_element_type=F32))
        return carry

    lax.fori_loop(0, NT, tile_gate, 0)

    for g, dy in enumerate(ROUND):
        y_from = lax.rem(row + 4 - dy, 4)
        received(g, lb.at[y_from, :, :, mate_low], rf.at[g])
        forward(8 + g, y_from, mate_low, (row, core_mate, depth))
    mate_other = lax.rem(other_low + 2, 4)
    for g, dy in enumerate(ROUND):
        y_from = lax.rem(row + 4 - dy, 4)
        received(4 + g, lb.at[y_from, :, :, other_low], rf.at[4 + g])
        received(8 + g, lb.at[y_from, :, :, mate_other], rf.at[8 + g])

    osc[:, :, (BASE + NJ) * HB : (BASE + NJ + 1) * HB, :] = jnp.zeros((4, 4, HB, 128), F32)
    relays, out_sends = [], []
    mine = x * 4 + row

    def block_of(stage, dy, dz):
        start = pl.multiple_of(BASE * HB + lax.rem(depth + dz, 4) * (NT * HB), HB)
        return osc[stage, lax.rem(row + dy, 4), pl.ds(start, MSG), :]

    def contract(stage, dx):
        x_from = lax.rem(x + 4 - dx, 4)
        for dy in ROUND:
            if (dx, dy) != (0, 0):
                y_from = lax.rem(row + 4 - dy, 4)
                n = NEAR.index((dx, dy))
                received(n, rb.at[x_from, y_from], rr.at[n])
        for h in range(HB):
            first = h * NJ // 16 * 16
            skew = h * NJ - first
            lhs = jnp.concatenate([rb[x_from, y, first : first + 64, :] for y in range(4)], axis=1)
            for half in range(2):
                rhs = jnp.concatenate(
                    [lb[half * 2 + q, h].reshape(512, NI) for q in range(2)], axis=1
                )
                sums = jnp.dot(lhs, rhs, preferred_element_type=F32)
                for q in range(2):
                    osc[stage, half * 2 + q, pl.ds((BASE - skew) * HB + h, 64, stride=HB), :] = sums[
                        :, q * NI : (q + 1) * NI
                    ]
        for side, dz in enumerate((1, 3)):
            for k, dy in enumerate(VIA[side]):
                av[stage, side, k] = block_of(stage, dy, 2).astype(BF16)
            copy = pltpu.make_async_remote_copy(
                src_ref=av.at[stage, side], dst_ref=ar.at[stage, side],
                send_sem=sa.at[stage * 2 + side], recv_sem=ra.at[stage * 2 + side],
                device_id=at(0, 0, dz), device_id_type=MESH,
            )
            copy.start()
            relays.append(copy)

    def distribute(stage, dx):
        x_from = lax.rem(x + 4 - dx, 4)
        for side in range(2):
            received(stage * 2 + side, ar.at[stage, side], ra.at[stage * 2 + side])
        for slot, dz in enumerate((1, 3, 0)):
            for dy in ROUND:
                block = block_of(stage, dy, dz)
                if slot < 2 and dy in VIA[slot]:
                    block = block + ar[stage, slot, VIA[slot].index(dy)].astype(F32)
                if (dx, dy, dz) == (0, 0, 0):
                    cb[slot, mine] = block.astype(BF16)
                    continue
                to_row, to_depth = lax.rem(row + dy, 4), lax.rem(depth + dz, 4)
                os_[stage, to_row, slot] = block.astype(BF16)
                n = len(out_sends)
                copy = pltpu.make_async_remote_copy(
                    src_ref=os_.at[stage, to_row, slot], dst_ref=cb.at[slot, mine],
                    send_sem=so.at[n], recv_sem=ro.at[n],
                    device_id=(to_row, x_from * 4 + low, to_depth), device_id_type=MESH,
                )
                copy.start()
                out_sends.append((dx, dy, slot, n, copy))

    for stage, dx in enumerate(ROUND):
        contract(stage, dx)
        if stage:
            distribute(stage - 1, ROUND[stage - 1])
    distribute(3, ROUND[3])

    for dx, dy, slot, n, copy in out_sends:
        x_at = lax.rem(x + dx, 4)
        y_at = lax.rem(row + 4 - dy, 4)
        received(n, cb.at[slot, x_at * 4 + y_at], ro.at[n])

    hg = jnp.broadcast_to(hgain[...], (128, 128)).T
    hb = jnp.broadcast_to(hbias[...], (128, 128)).T
    weight = wo[...]

    def finish(j, sums):
        centre = jnp.mean(sums, axis=0, keepdims=True)
        shifted = sums - centre
        spread = jnp.mean(shifted * shifted, axis=0, keepdims=True)
        hidden = (shifted * lax.rsqrt(spread + EPSILON) * hg + hb).astype(BF16)
        projected = lax.dot_general(
            hidden, weight, (((0,), (0,)), ((), ())), preferred_element_type=F32
        )
        out[j] = (gate[j] * projected).astype(BF16)

    def pair_of_columns(p, carry):
        rows = pl.ds(pl.multiple_of(p * 16, 16), 16)
        total = cb[0, :, rows, :].astype(F32)
        for z in range(1, 3):
            total = total + cb[z, :, rows, :].astype(F32)
        finish(p * 2, total[:, :HB].reshape(128, NI))

        @pl.when(p < JPAD // 2 - 1)
        def _():
            finish(p * 2 + 1, total[:, HB:].reshape(128, NI))

        return carry

    lax.fori_loop(0, JPAD // 2, pair_of_columns, 0)

    for copy in list(left_sends.values()) + list(right_sends.values()) + forwards + relays:
        copy.wait_send()
    for item in out_sends:
        item[4].wait_send()


def per_device(
    left_pair, right_pair, pair_tile, row_flags, column_flags, key_flags,
    input_gain, input_bias, left_gate_weight, left_value_weight,
    right_gate_weight, right_value_weight, hidden_gain, hidden_bias,
    output_gate_weight, output_weight,
):
    dma = pltpu.SemaphoreType.DMA
    operands = (
        left_pair.reshape(NI * NM, 128),
        right_pair.reshape(NJ * NK, 128),
        pair_tile.transpose(1, 0, 2),
        row_flags.reshape(1, NI),
        column_flags,
        key_flags,
        key_flags,
        input_gain.reshape(1, 128),
        input_bias.reshape(1, 128),
        left_gate_weight, left_value_weight, right_gate_weight, right_value_weight,
        hidden_gain.reshape(1, 128),
        hidden_bias.reshape(1, 128),
        output_gate_weight, output_weight,
    )
    held = [
        pltpu.SMEM(a.shape, a.dtype) if n in (4, 5) else pltpu.VMEM(a.shape, a.dtype)
        for n, a in enumerate(operands)
    ]
    result = pl.pallas_call(
        kernel,
        out_shape=jax.ShapeDtypeStruct((NT, NI, 128), BF16),
        in_specs=[pl.BlockSpec(memory_space=pltpu.HBM)] * len(operands),
        out_specs=pl.BlockSpec(memory_space=pltpu.VMEM),
        scratch_shapes=held + [
            pltpu.VMEM((NI * NM, 128), F32),
            pltpu.VMEM((16 * HB * NM, 128), F32),
            pltpu.VMEM((16 * HB * NJ, 128), F32),
            pltpu.VMEM((16, HB, NM, NI), BF16),
            pltpu.VMEM((4, HB, 4, 4, NM, NI), BF16),
            pltpu.VMEM((16, HB * NJ, NK), BF16),
            pltpu.VMEM((4, 4, HB * NJ, NK), BF16),
            pltpu.VMEM((4, 4, SLOTS * HB, 128), F32),
            pltpu.VMEM((4, 2, 2, MSG, 128), BF16),
            pltpu.VMEM((4, 2, 2, MSG, 128), BF16),
            pltpu.VMEM((4, 4, 3, MSG, 128), BF16),
            pltpu.VMEM((3, 16, MSG, 128), BF16),
            pltpu.VMEM((NT, NI, 128), F32),
            dma((16,)), dma((16,)), dma((16,)), dma((16,)),
            dma((12,)), dma((12,)), dma((8,)), dma((8,)),
            dma((47,)), dma((47,)), dma((1,)), dma((17,)),
        ],
        compiler_params=pltpu.CompilerParams(
            collective_id=0, has_side_effects=True, vmem_limit_bytes=60 * 2**20
        ),
        name="triangle",
    )(*operands)
    return result.transpose(1, 0, 2)


def solution(mesh):
    in_specs = (
        P("row", "depth", "col", None),
        P("col", "depth", "row", None),
        P("row", ("col", "depth"), None),
        P("row"),
        P("col"),
    ) + (P(),) * 11
    return jax.shard_map(
        per_device,
        mesh=mesh,
        in_specs=in_specs,
        out_specs=P("row", ("col", "depth"), None),
        check_vma=False,
    )
```

```python
import functools

import jax
import jax.numpy as jnp
from jax import lax
from jax.experimental import pallas as pl
from jax.experimental.pallas import tpu as pltpu
from jax.sharding import PartitionSpec as P

EPSILON = 1e-05
MESH = pl.DeviceIdType.MESH
F32 = jnp.float32
BF16 = jnp.bfloat16

NI, NM, NJ, NK, NT = 128, 32, 52, 128, 13
HB = 8
JPAD = NT + 1
MSG = JPAD * HB
SLOTS = 80
BASE = 16

ROUND = (2, 1, 3, 0)
VIA = ((2, 0), (1, 3))
def hops(offset):
    return sum(min(d, 4 - d) for d in offset)


STAGED = [(dx, dy) for dx in ROUND for dy in ROUND]
NEAR = sorted([(dx, dy) for dx in ROUND for dy in ROUND], key=hops, reverse=True)
DIRECT = [offset for offset in NEAR if hops(offset) <= 0]


LOAD_ORDER = (0, 7, 8, 9, 10, 3, 5, 1, 11, 12, 4, 6, 2, 15, 13, 14, 16)


def normalise(values):
    values = values.astype(F32)
    centre = jnp.mean(values, axis=-1, keepdims=True)
    shifted = values - centre
    spread = jnp.mean(shifted * shifted, axis=-1, keepdims=True)
    return shifted * lax.rsqrt(spread + EPSILON)


def sigmoid(values):
    return 0.5 * jnp.tanh(0.5 * values) + 0.5


def dot_nt(left, right):
    return lax.dot_general(left, right, (((1,), (1,)), ((), ())), preferred_element_type=F32)


def kernel(*refs):
    sources, refs = refs[:17], refs[17:]
    out, refs = refs[0], refs[1:]
    held, refs = refs[:17], refs[17:]
    (
        xl, xr, xt, row_flags, column_flags, key_scalars, key_rows,
        gain, bias, wlg, wlv, wrg, wrv, hgain, hbias, wog, wo,
    ) = held
    (
        nl, tl, tr, ls, lb, rs, rb, osc, av, ar, os_, cb, gate,
        sl, rl, sr, rr, sz, rz, sc, rc, sa, ra, so, ro, cs, loads,
    ) = refs
    pending = [
        pltpu.make_async_copy(src, dst, loads.at[n])
        for n, (src, dst) in enumerate(zip(sources, held))
    ]
    for n in LOAD_ORDER:
        pending[n].start()

    def loaded(*numbers):
        for n in numbers:
            pending[n].wait()

    row = lax.axis_index("row")
    col = lax.axis_index("col")
    depth = lax.axis_index("depth")
    x = lax.div(col, 4)
    low = lax.rem(col, 4)
    core_mate = x * 4 + low + 1 - 2 * lax.rem(low, 2)
    mate_low = lax.rem(low + 2, 4)
    z_mate = x * 4 + mate_low
    other_low = low + 1 - 2 * lax.rem(low, 2)

    def at(dx, dy, dz=0):
        return (
            lax.rem(row + dy, 4),
            lax.rem(x + dx, 4) * 4 + low,
            lax.rem(depth + dz, 4),
        )

    barrier = pltpu.get_barrier_semaphore()
    peers = [at(dx, dy, dz) for dz in (0, 1, 3) for dx, dy in NEAR if (dx, dy, dz) != (0, 0, 0)]
    peers.append((row, core_mate, depth))
    for offset in DIRECT:
        to_row, to_col, _ = at(*offset)
        peers.append((to_row, to_col - low + mate_low, depth))
    for peer in peers:
        pl.semaphore_signal(barrier, inc=1, device_id=peer, device_id_type=MESH)

    loaded(0, 7, 8, 9, 10, 3, 5)
    gains, biases = gain[...], bias[...]

    def left_norm(step, carry):
        rows = pl.ds(pl.multiple_of(step * 512, 512), 512)
        nl[rows, :] = normalise(xl[rows, :]) * gains + biases
        return carry

    lax.fori_loop(0, NI * NM // 512, left_norm, 0)
    w_left = jnp.concatenate([wlg[...], wlv[...]], axis=1).astype(F32).T.astype(BF16)
    row_mask = row_flags[...].astype(F32)

    def left_act(step, carry):
        xs = jnp.concatenate(
            [nl[pl.ds(step * 8 + mm, NI, stride=NM), :] for mm in range(8)], axis=0
        ).astype(BF16)
        both = dot_nt(w_left, xs)
        act = sigmoid(both[:128]) * both[128:]
        for mm in range(8):
            key = key_scalars[depth, col * NM + step * 8 + mm].astype(F32)
            part = act[:, mm * NI : (mm + 1) * NI] * (row_mask * key)
            for d in range(16):
                tl[pl.ds(d * HB * NM + step * 8 + mm, HB, stride=NM), :] = part[d * HB : (d + 1) * HB]
        return carry

    lax.fori_loop(0, NM // 8, left_act, 0)

    pl.semaphore_wait(barrier, len(peers))

    def owner(dx, dy):
        return lax.rem(x + dx, 4) * 4 + lax.rem(row + dy, 4)

    sends = []

    def send(src, dst, send_sem, recv_sem, device):
        copy = pltpu.make_async_remote_copy(
            src_ref=src, dst_ref=dst, send_sem=send_sem, recv_sem=recv_sem,
            device_id=device, device_id_type=MESH,
        )
        copy.start()
        sends.append(copy)

    def received(dst, sem):
        pltpu.make_async_remote_copy(
            src_ref=dst, dst_ref=dst, send_sem=sem, recv_sem=sem,
            device_id=at(1, 0), device_id_type=MESH,
        ).wait_recv()

    def source(dx, dy):
        return lax.rem(x + 4 - dx, 4), lax.rem(row + 4 - dy, 4)

    for n, (dx, dy) in enumerate(NEAR):
        d = owner(dx, dy)
        rows = pl.ds(pl.multiple_of(d * HB * NM, HB * NM), HB * NM)
        ls[d] = tl[rows, :].astype(BF16).reshape(HB, NM, NI)
        target = lb.at[row, :, x, low]
        if (dx, dy) == (0, 0):
            pltpu.make_async_copy(ls.at[d], target, cs.at[0]).start()
            send(ls.at[d], target, sc.at[n], rc.at[n], (row, core_mate, depth))
        else:
            send(ls.at[d], target, sl.at[n], rl.at[n], at(dx, dy))
        if (dx, dy) in DIRECT:
            to_row, to_col, _ = at(dx, dy)
            send(ls.at[d], target, sz.at[n], rz.at[n], (to_row, to_col - low + mate_low, depth))

    loaded(1, 11, 12, 4, 6)
    w_right = jnp.concatenate([wrg[...], wrv[...]], axis=1).astype(F32).T.astype(BF16)
    key_block = key_rows[:, pl.ds(pl.multiple_of(row * NK, NK), NK)].astype(F32)
    here = lax.broadcasted_iota(jnp.int32, (4, NK), 0) == depth
    key_mask = jnp.sum(jnp.where(here, key_block, 0.0), axis=0, keepdims=True)

    def right_act(step, carry):
        rows = pl.ds(pl.multiple_of(step * 1664, 128), 1664)
        xs = (normalise(xr[rows, :]) * gains + biases).astype(BF16)
        both = dot_nt(w_right, xs)
        act = sigmoid(both[:128]) * both[128:]
        for jj in range(13):
            flag = column_flags[step * 13 + jj].astype(F32)
            part = act[:, jj * NK : (jj + 1) * NK] * (key_mask * flag)
            for d in range(16):
                tr[pl.ds(d * HB * NJ + step * 13 + jj, HB, stride=NJ), :] = part[d * HB : (d + 1) * HB]
        return carry

    lax.fori_loop(0, NJ // 13, right_act, 0)

    for n, (dx, dy) in enumerate(STAGED):
        d = owner(dx, dy)
        rows = pl.ds(pl.multiple_of(d * HB * NJ, HB * NJ), HB * NJ)
        if (dx, dy) == (0, 0):
            rb[x, row] = tr[rows, :].astype(BF16)
            continue
        rs[d] = tr[rows, :].astype(BF16)
        send(rs.at[d], rb.at[x, row], sr.at[n], rr.at[n], at(dx, dy))

    pltpu.make_async_copy(ls.at[owner(0, 0)], lb.at[row, :, x, low], cs.at[0]).wait()
    for n, offset in enumerate(NEAR):
        if offset == (0, 0):
            continue
        x_from, y_from = source(*offset)
        part = lb.at[y_from, :, x_from, low]
        received(part, rl.at[n])
        if offset not in DIRECT:
            send(part, part, sz.at[n], rz.at[n], (row, z_mate, depth))
        send(part, part, sc.at[n], rc.at[n], (row, core_mate, depth))

    loaded(2, 15, 13, 14, 16)
    tile_weight = wog[...]

    def tile_gate(j, carry):
        normed = (normalise(xt[j]) * gains + biases).astype(BF16)
        gate[j] = sigmoid(jnp.dot(normed, tile_weight, preferred_element_type=F32))
        return carry

    lax.fori_loop(0, NT, tile_gate, 0)

    for n, offset in reversed(list(enumerate(NEAR))):
        x_from, y_from = source(*offset)
        part = lb.at[y_from, :, x_from, mate_low]
        received(part, rz.at[n])
        send(part, part, sc.at[16 + n], rc.at[16 + n], (row, core_mate, depth))
    mate_other = lax.rem(other_low + 2, 4)
    for n, offset in enumerate(NEAR):
        x_from, y_from = source(*offset)
        received(lb.at[y_from, :, x_from, other_low], rc.at[n])
        received(lb.at[y_from, :, x_from, mate_other], rc.at[16 + n])

    osc[:, :, (BASE + NJ) * HB : (BASE + NJ + 1) * HB, :] = jnp.zeros((4, 4, HB, 128), F32)
    out_sends = []
    mine = x * 4 + row

    def block_of(stage, dy, dz):
        start = pl.multiple_of(BASE * HB + lax.rem(depth + dz, 4) * (NT * HB), HB)
        return osc[stage, lax.rem(row + dy, 4), pl.ds(start, MSG), :]

    def contract(stage, dx):
        x_from = lax.rem(x + 4 - dx, 4)
        for dy in ROUND:
            if (dx, dy) != (0, 0):
                y_from = lax.rem(row + 4 - dy, 4)
                received(rb.at[x_from, y_from], rr.at[STAGED.index((dx, dy))])
        for h in range(HB):
            first = h * NJ // 16 * 16
            skew = h * NJ - first
            lhs = jnp.concatenate([rb[x_from, y, first : first + 64, :] for y in range(4)], axis=1)
            for half in range(2):
                rhs = jnp.concatenate(
                    [lb[half * 2 + q, h].reshape(512, NI) for q in range(2)], axis=1
                )
                sums = jnp.dot(lhs, rhs, preferred_element_type=F32)
                for q in range(2):
                    osc[stage, half * 2 + q, pl.ds((BASE - skew) * HB + h, 64, stride=HB), :] = sums[
                        :, q * NI : (q + 1) * NI
                    ]
        for side, dz in enumerate((1, 3)):
            for k, dy in enumerate(VIA[side]):
                av[stage, side, k] = block_of(stage, dy, 2).astype(BF16)
            sems = sa.at[stage * 2 + side], ra.at[stage * 2 + side]
            send(av.at[stage, side], ar.at[stage, side], *sems, at(0, 0, dz))

    def distribute(stage, dx):
        x_from = lax.rem(x + 4 - dx, 4)
        for side in range(2):
            received(ar.at[stage, side], ra.at[stage * 2 + side])
        for slot, dz in enumerate((1, 3, 0)):
            for dy in ROUND:
                block = block_of(stage, dy, dz)
                if slot < 2 and dy in VIA[slot]:
                    block = block + ar[stage, slot, VIA[slot].index(dy)].astype(F32)
                if (dx, dy, dz) == (0, 0, 0):
                    cb[slot, mine] = block.astype(BF16)
                    continue
                to_row, to_depth = lax.rem(row + dy, 4), lax.rem(depth + dz, 4)
                os_[stage, to_row, slot] = block.astype(BF16)
                n = len(out_sends)
                target = (to_row, x_from * 4 + low, to_depth)
                send(os_.at[stage, to_row, slot], cb.at[slot, mine], so.at[n], ro.at[n], target)
                out_sends.append((dx, dy, slot))

    for stage, dx in enumerate(ROUND):
        contract(stage, dx)
        if stage:
            distribute(stage - 1, ROUND[stage - 1])
    distribute(3, ROUND[3])

    for n, (dx, dy, slot) in enumerate(out_sends):
        x_at = lax.rem(x + dx, 4)
        y_at = lax.rem(row + 4 - dy, 4)
        received(cb.at[slot, x_at * 4 + y_at], ro.at[n])

    hg = jnp.broadcast_to(hgain[...], (128, 128)).T
    hb = jnp.broadcast_to(hbias[...], (128, 128)).T
    weight = wo[...]

    def finish(j, sums):
        centre = jnp.mean(sums, axis=0, keepdims=True)
        shifted = sums - centre
        spread = jnp.mean(shifted * shifted, axis=0, keepdims=True)
        hidden = (shifted * lax.rsqrt(spread + EPSILON) * hg + hb).astype(BF16)
        projected = lax.dot_general(
            hidden, weight, (((0,), (0,)), ((), ())), preferred_element_type=F32
        )
        out[j] = (gate[j] * projected).astype(BF16)

    for p in range(JPAD // 2):
        rows = slice(p * 16, p * 16 + 16)
        total = cb[0, :, rows, :].astype(F32)
        for z in range(1, 3):
            total = total + cb[z, :, rows, :].astype(F32)
        finish(p * 2, total[:, :HB].reshape(128, NI))
        if p < JPAD // 2 - 1:
            finish(p * 2 + 1, total[:, HB:].reshape(128, NI))

    for copy in sends:
        copy.wait_send()


def per_device(
    left_pair, right_pair, pair_tile, row_flags, column_flags, key_flags,
    input_gain, input_bias, left_gate_weight, left_value_weight,
    right_gate_weight, right_value_weight, hidden_gain, hidden_bias,
    output_gate_weight, output_weight,
):
    dma = pltpu.SemaphoreType.DMA
    operands = (
        left_pair.reshape(NI * NM, 128),
        right_pair.reshape(NJ * NK, 128),
        pair_tile.transpose(1, 0, 2),
        row_flags.reshape(1, NI),
        column_flags,
        key_flags,
        key_flags,
        input_gain.reshape(1, 128),
        input_bias.reshape(1, 128),
        left_gate_weight, left_value_weight, right_gate_weight, right_value_weight,
        hidden_gain.reshape(1, 128),
        hidden_bias.reshape(1, 128),
        output_gate_weight, output_weight,
    )
    held = [
        pltpu.SMEM(a.shape, a.dtype) if n in (4, 5) else pltpu.VMEM(a.shape, a.dtype)
        for n, a in enumerate(operands)
    ]
    result = pl.pallas_call(
        kernel,
        out_shape=jax.ShapeDtypeStruct((NT, NI, 128), BF16),
        in_specs=[pl.BlockSpec(memory_space=pltpu.HBM)] * len(operands),
        out_specs=pl.BlockSpec(memory_space=pltpu.VMEM),
        scratch_shapes=held + [
            pltpu.VMEM((NI * NM, 128), F32),
            pltpu.VMEM((16 * HB * NM, 128), F32),
            pltpu.VMEM((16 * HB * NJ, 128), F32),
            pltpu.VMEM((16, HB, NM, NI), BF16),
            pltpu.VMEM((4, HB, 4, 4, NM, NI), BF16),
            pltpu.VMEM((16, HB * NJ, NK), BF16),
            pltpu.VMEM((4, 4, HB * NJ, NK), BF16),
            pltpu.VMEM((4, 4, SLOTS * HB, 128), F32),
            pltpu.VMEM((4, 2, 2, MSG, 128), BF16),
            pltpu.VMEM((4, 2, 2, MSG, 128), BF16),
            pltpu.VMEM((4, 4, 3, MSG, 128), BF16),
            pltpu.VMEM((3, 16, MSG, 128), BF16),
            pltpu.VMEM((NT, NI, 128), F32),
            dma((16,)), dma((16,)), dma((16,)), dma((16,)),
            dma((16,)), dma((16,)), dma((32,)), dma((32,)), dma((8,)), dma((8,)),
            dma((47,)), dma((47,)), dma((1,)), dma((17,)),
        ],
        compiler_params=pltpu.CompilerParams(
            collective_id=0, has_side_effects=True, vmem_limit_bytes=60 * 2**20
        ),
        name="triangle",
    )(*operands)
    return result.transpose(1, 0, 2)


def solution(mesh):
    in_specs = (
        P("row", "depth", "col", None),
        P("col", "depth", "row", None),
        P("row", ("col", "depth"), None),
        P("row"),
        P("col"),
    ) + (P(),) * 11
    return jax.shard_map(
        per_device,
        mesh=mesh,
        in_specs=in_specs,
        out_specs=P("row", ("col", "depth"), None),
        check_vma=False,
    )
```

```python
import functools

import jax
import jax.numpy as jnp
from jax import lax
from jax.experimental import pallas as pl
from jax.experimental.pallas import tpu as pltpu
from jax.sharding import PartitionSpec as P

EPSILON = 1e-05
MESH = pl.DeviceIdType.MESH
F32 = jnp.float32
BF16 = jnp.bfloat16

NI, NM, NJ, NK, NT = 128, 32, 52, 128, 13
HB = 8
JPAD = NT + 1
MSG = JPAD * HB
SLOTS = 80
BASE = 16

LEFT, ACROSS, CORE, CORE_ACROSS, RIGHT, RELAY, OUT = range(7)

ROUND = (2, 1, 3, 0)
VIA = ((2, 0), (1, 3))
def hops(offset):
    return sum(min(d, 4 - d) for d in offset)


STAGED = [(dx, dy) for dx in ROUND for dy in ROUND]
NEAR = sorted([(dx, dy) for dx in ROUND for dy in ROUND], key=hops, reverse=True)
DIRECT = [offset for offset in NEAR if hops(offset) <= 0]


LOAD_ORDER = (0, 7, 8, 9, 10, 3, 5, 1, 11, 12, 4, 6, 2, 15, 13, 14, 16)


def normalise(values):
    values = values.astype(F32)
    centre = jnp.mean(values, axis=-1, keepdims=True)
    shifted = values - centre
    spread = jnp.mean(shifted * shifted, axis=-1, keepdims=True)
    return shifted * lax.rsqrt(spread + EPSILON)


def sigmoid(values):
    return 0.5 * jnp.tanh(0.5 * values) + 0.5


def dot_nt(left, right):
    return lax.dot_general(left, right, (((1,), (1,)), ((), ())), preferred_element_type=F32)


def kernel(*refs):
    sources, refs = refs[:17], refs[17:]
    out, refs = refs[0], refs[1:]
    held, refs = refs[:17], refs[17:]
    (
        xl, xr, xt, row_flags, column_flags, key_scalars, key_rows,
        gain, bias, wlg, wlv, wrg, wrv, hgain, hbias, wog, wo,
    ) = held
    (
        nl, tl, tr, ls, lb, rs, rb, osc, av, ar, os_, cb, gate,
        sent, rl, rr, rz, rc, ra, ro, cs, loads,
    ) = refs
    pending = [
        pltpu.make_async_copy(src, dst, loads.at[n])
        for n, (src, dst) in enumerate(zip(sources, held))
    ]
    for n in LOAD_ORDER:
        pending[n].start()

    def loaded(*numbers):
        for n in numbers:
            pending[n].wait()

    row = lax.axis_index("row")
    col = lax.axis_index("col")
    depth = lax.axis_index("depth")
    x = lax.div(col, 4)
    low = lax.rem(col, 4)
    core_mate = x * 4 + low + 1 - 2 * lax.rem(low, 2)
    mate_low = lax.rem(low + 2, 4)
    z_mate = x * 4 + mate_low
    other_low = low + 1 - 2 * lax.rem(low, 2)

    def at(dx, dy, dz=0):
        return (
            lax.rem(row + dy, 4),
            lax.rem(x + dx, 4) * 4 + low,
            lax.rem(depth + dz, 4),
        )

    barrier = pltpu.get_barrier_semaphore()
    peers = [at(dx, dy, dz) for dz in (0, 1, 3) for dx, dy in NEAR if (dx, dy, dz) != (0, 0, 0)]
    peers.append((row, core_mate, depth))
    for offset in DIRECT:
        to_row, to_col, _ = at(*offset)
        peers.append((to_row, to_col - low + mate_low, depth))
    for peer in peers:
        pl.semaphore_signal(barrier, inc=1, device_id=peer, device_id_type=MESH)

    loaded(0, 7, 8, 9, 10, 3, 5)
    gains, biases = gain[...], bias[...]

    def left_norm(step, carry):
        rows = pl.ds(pl.multiple_of(step * 512, 512), 512)
        nl[rows, :] = normalise(xl[rows, :]) * gains + biases
        return carry

    lax.fori_loop(0, NI * NM // 512, left_norm, 0)
    w_left = jnp.concatenate([wlg[...], wlv[...]], axis=1).astype(F32).T.astype(BF16)
    row_mask = row_flags[...].astype(F32)

    def left_act(step, carry):
        xs = jnp.concatenate(
            [nl[pl.ds(step * 8 + mm, NI, stride=NM), :] for mm in range(8)], axis=0
        ).astype(BF16)
        both = dot_nt(w_left, xs)
        act = sigmoid(both[:128]) * both[128:]
        for mm in range(8):
            key = key_scalars[depth, col * NM + step * 8 + mm].astype(F32)
            part = act[:, mm * NI : (mm + 1) * NI] * (row_mask * key)
            for d in range(16):
                tl[pl.ds(d * HB * NM + step * 8 + mm, HB, stride=NM), :] = part[d * HB : (d + 1) * HB]
        return carry

    lax.fori_loop(0, NM // 8, left_act, 0)

    pl.semaphore_wait(barrier, len(peers))

    def owner(dx, dy):
        return lax.rem(x + dx, 4) * 4 + lax.rem(row + dy, 4)

    def send(src, dst, kind, recv_sem, device):
        pltpu.make_async_remote_copy(
            src_ref=src, dst_ref=dst, send_sem=sent.at[kind], recv_sem=recv_sem,
            device_id=device, device_id_type=MESH,
        ).start()

    def received(dst, sem):
        pltpu.make_async_remote_copy(
            src_ref=dst, dst_ref=dst, send_sem=sem, recv_sem=sem,
            device_id=at(1, 0), device_id_type=MESH,
        ).wait_recv()

    def source(dx, dy):
        return lax.rem(x + 4 - dx, 4), lax.rem(row + 4 - dy, 4)

    for n, (dx, dy) in enumerate(NEAR):
        d = owner(dx, dy)
        rows = pl.ds(pl.multiple_of(d * HB * NM, HB * NM), HB * NM)
        ls[d] = tl[rows, :].astype(BF16).reshape(HB, NM, NI)
        target = lb.at[row, :, x, low]
        if (dx, dy) == (0, 0):
            pltpu.make_async_copy(ls.at[d], target, cs.at[0]).start()
            send(ls.at[d], target, CORE, rc.at[0], (row, core_mate, depth))
        else:
            send(ls.at[d], target, LEFT, rl.at[n], at(dx, dy))
        if (dx, dy) in DIRECT:
            to_row, to_col, _ = at(dx, dy)
            send(ls.at[d], target, ACROSS, rz.at[n], (to_row, to_col - low + mate_low, depth))

    loaded(1, 11, 12, 4, 6)
    w_right = jnp.concatenate([wrg[...], wrv[...]], axis=1).astype(F32).T.astype(BF16)
    key_block = key_rows[:, pl.ds(pl.multiple_of(row * NK, NK), NK)].astype(F32)
    here = lax.broadcasted_iota(jnp.int32, (4, NK), 0) == depth
    key_mask = jnp.sum(jnp.where(here, key_block, 0.0), axis=0, keepdims=True)

    def right_act(step, carry):
        rows = pl.ds(pl.multiple_of(step * 1664, 128), 1664)
        xs = (normalise(xr[rows, :]) * gains + biases).astype(BF16)
        both = dot_nt(w_right, xs)
        act = sigmoid(both[:128]) * both[128:]
        for jj in range(13):
            flag = column_flags[step * 13 + jj].astype(F32)
            part = act[:, jj * NK : (jj + 1) * NK] * (key_mask * flag)
            for d in range(16):
                tr[pl.ds(d * HB * NJ + step * 13 + jj, HB, stride=NJ), :] = part[d * HB : (d + 1) * HB]
        return carry

    lax.fori_loop(0, NJ // 13, right_act, 0)

    for n, (dx, dy) in enumerate(STAGED):
        d = owner(dx, dy)
        rows = pl.ds(pl.multiple_of(d * HB * NJ, HB * NJ), HB * NJ)
        if (dx, dy) == (0, 0):
            rb[x, row] = tr[rows, :].astype(BF16)
            continue
        rs[d] = tr[rows, :].astype(BF16)
        send(rs.at[d], rb.at[x, row], RIGHT, rr.at[ROUND.index(dx)], at(dx, dy))

    pltpu.make_async_copy(ls.at[owner(0, 0)], lb.at[row, :, x, low], cs.at[0]).wait()
    for n, offset in enumerate(NEAR):
        if offset == (0, 0):
            continue
        x_from, y_from = source(*offset)
        part = lb.at[y_from, :, x_from, low]
        received(part, rl.at[n])
        if offset not in DIRECT:
            send(part, part, ACROSS, rz.at[n], (row, z_mate, depth))
        send(part, part, CORE, rc.at[0], (row, core_mate, depth))

    for n, offset in reversed(list(enumerate(NEAR))):
        x_from, y_from = source(*offset)
        part = lb.at[y_from, :, x_from, mate_low]
        received(part, rz.at[n])
        send(part, part, CORE_ACROSS, rc.at[1], (row, core_mate, depth))
    mate_other = lax.rem(other_low + 2, 4)
    received(lb.at[:, :, :, other_low], rc.at[0])
    received(lb.at[:, :, :, mate_other], rc.at[1])

    osc[:, :, (BASE + NJ) * HB : (BASE + NJ + 1) * HB, :] = jnp.zeros((4, 4, HB, 128), F32)
    out_sends = []
    mine = x * 4 + row

    def block_of(stage, dy, dz):
        start = pl.multiple_of(BASE * HB + lax.rem(depth + dz, 4) * (NT * HB), HB)
        return osc[stage, lax.rem(row + dy, 4), pl.ds(start, MSG), :]

    def contract(stage, dx):
        x_from = lax.rem(x + 4 - dx, 4)
        received(rb.at[x_from] if dx else rb.at[x_from, pl.ds(0, 3)], rr.at[stage])
        for h in range(HB):
            first = h * NJ // 16 * 16
            skew = h * NJ - first
            lhs = jnp.concatenate([rb[x_from, y, first : first + 64, :] for y in range(4)], axis=1)
            for half in range(2):
                rhs = jnp.concatenate(
                    [lb[half * 2 + q, h].reshape(512, NI) for q in range(2)], axis=1
                )
                sums = jnp.dot(lhs, rhs, preferred_element_type=F32)
                for q in range(2):
                    osc[stage, half * 2 + q, pl.ds((BASE - skew) * HB + h, 64, stride=HB), :] = sums[
                        :, q * NI : (q + 1) * NI
                    ]
        for side, dz in enumerate((1, 3)):
            for k, dy in enumerate(VIA[side]):
                av[stage, side, k] = block_of(stage, dy, 2).astype(BF16)
            send(av.at[stage, side], ar.at[stage, side], RELAY, ra.at[stage], at(0, 0, dz))

    def distribute(stage, dx):
        x_from = lax.rem(x + 4 - dx, 4)
        received(ar.at[stage], ra.at[stage])
        for slot, dz in enumerate((1, 3, 0)):
            for dy in ROUND:
                block = block_of(stage, dy, dz)
                if slot < 2 and dy in VIA[slot]:
                    block = block + ar[stage, slot, VIA[slot].index(dy)].astype(F32)
                if (dx, dy, dz) == (0, 0, 0):
                    cb[slot * 16 + mine] = block.astype(BF16)
                    continue
                to_row, to_depth = lax.rem(row + dy, 4), lax.rem(depth + dz, 4)
                n = len(out_sends)
                os_[n] = block.astype(BF16)
                target = (to_row, x_from * 4 + low, to_depth)
                send(os_.at[n], cb.at[slot * 16 + mine], OUT, ro.at[0], target)
                out_sends.append((dx, dy, slot))

    for stage, dx in enumerate(ROUND):
        contract(stage, dx)
    for stage, dx in enumerate(ROUND):
        distribute(stage, dx)

    loaded(2, 15, 13, 14, 16)
    tile_weight = wog[...]

    def tile_gate(j, carry):
        normed = (normalise(xt[j]) * gains + biases).astype(BF16)
        gate[j] = sigmoid(jnp.dot(normed, tile_weight, preferred_element_type=F32))
        return carry

    lax.fori_loop(0, NT, tile_gate, 0)

    received(cb.at[pl.ds(0, 47)], ro.at[0])

    hg = jnp.broadcast_to(hgain[...], (128, 128)).T
    hb = jnp.broadcast_to(hbias[...], (128, 128)).T
    weight = wo[...]

    def finish(j, sums):
        centre = jnp.mean(sums, axis=0, keepdims=True)
        shifted = sums - centre
        spread = jnp.mean(shifted * shifted, axis=0, keepdims=True)
        hidden = (shifted * lax.rsqrt(spread + EPSILON) * hg + hb).astype(BF16)
        projected = lax.dot_general(
            hidden, weight, (((0,), (0,)), ((), ())), preferred_element_type=F32
        )
        out[j] = (gate[j] * projected).astype(BF16)

    for p in range(JPAD // 2):
        rows = slice(p * 16, p * 16 + 16)
        total = cb[0:16, rows, :].astype(F32)
        for z in range(1, 3):
            total = total + cb[z * 16 : z * 16 + 16, rows, :].astype(F32)
        finish(p * 2, total[:, :HB].reshape(128, NI))
        if p < JPAD // 2 - 1:
            finish(p * 2 + 1, total[:, HB:].reshape(128, NI))

    for kind, part in (
        (LEFT, ls.at[pl.ds(0, 15)]), (ACROSS, ls), (CORE, ls), (CORE_ACROSS, ls),
        (RIGHT, rs.at[pl.ds(0, 15)]), (RELAY, av), (OUT, os_),
    ):
        pltpu.make_async_remote_copy(
            src_ref=part, dst_ref=part, send_sem=sent.at[kind], recv_sem=sent.at[kind],
            device_id=at(1, 0), device_id_type=MESH,
        ).wait_send()


def per_device(
    left_pair, right_pair, pair_tile, row_flags, column_flags, key_flags,
    input_gain, input_bias, left_gate_weight, left_value_weight,
    right_gate_weight, right_value_weight, hidden_gain, hidden_bias,
    output_gate_weight, output_weight,
):
    dma = pltpu.SemaphoreType.DMA
    operands = (
        left_pair.reshape(NI * NM, 128),
        right_pair.reshape(NJ * NK, 128),
        pair_tile.transpose(1, 0, 2),
        row_flags.reshape(1, NI),
        column_flags,
        key_flags,
        key_flags,
        input_gain.reshape(1, 128),
        input_bias.reshape(1, 128),
        left_gate_weight, left_value_weight, right_gate_weight, right_value_weight,
        hidden_gain.reshape(1, 128),
        hidden_bias.reshape(1, 128),
        output_gate_weight, output_weight,
    )
    held = [
        pltpu.SMEM(a.shape, a.dtype) if n in (4, 5) else pltpu.VMEM(a.shape, a.dtype)
        for n, a in enumerate(operands)
    ]
    result = pl.pallas_call(
        kernel,
        out_shape=jax.ShapeDtypeStruct((NT, NI, 128), BF16),
        in_specs=[pl.BlockSpec(memory_space=pltpu.HBM)] * len(operands),
        out_specs=pl.BlockSpec(memory_space=pltpu.VMEM),
        scratch_shapes=held + [
            pltpu.VMEM((NI * NM, 128), F32),
            pltpu.VMEM((16 * HB * NM, 128), F32),
            pltpu.VMEM((16 * HB * NJ, 128), F32),
            pltpu.VMEM((16, HB, NM, NI), BF16),
            pltpu.VMEM((4, HB, 4, 4, NM, NI), BF16),
            pltpu.VMEM((16, HB * NJ, NK), BF16),
            pltpu.VMEM((4, 4, HB * NJ, NK), BF16),
            pltpu.VMEM((4, 4, SLOTS * HB, 128), F32),
            pltpu.VMEM((4, 2, 2, MSG, 128), BF16),
            pltpu.VMEM((4, 2, 2, MSG, 128), BF16),
            pltpu.VMEM((47, MSG, 128), BF16),
            pltpu.VMEM((48, MSG, 128), BF16),
            pltpu.VMEM((NT, NI, 128), F32),
            dma((7,)), dma((15,)), dma((4,)), dma((16,)), dma((2,)), dma((4,)),
            dma((1,)), dma((1,)), dma((17,)),
        ],
        compiler_params=pltpu.CompilerParams(
            collective_id=0, has_side_effects=True, vmem_limit_bytes=60 * 2**20
        ),
        name="triangle",
    )(*operands)
    return result.transpose(1, 0, 2)


def solution(mesh):
    in_specs = (
        P("row", "depth", "col", None),
        P("col", "depth", "row", None),
        P("row", ("col", "depth"), None),
        P("row"),
        P("col"),
    ) + (P(),) * 11
    return jax.shard_map(
        per_device,
        mesh=mesh,
        in_specs=in_specs,
        out_specs=P("row", ("col", "depth"), None),
        check_vma=False,
    )
```

```python
import functools

import jax
import jax.numpy as jnp
from jax import lax
from jax.experimental import pallas as pl
from jax.experimental.pallas import tpu as pltpu
from jax.sharding import PartitionSpec as P

EPSILON = 1e-05
MESH = pl.DeviceIdType.MESH
F32 = jnp.float32
BF16 = jnp.bfloat16

NI, NM, NJ, NK, NT = 128, 32, 52, 128, 13
HB = 8
JPAD = NT + 1
MSG = JPAD * HB
SLOTS = 80
BASE = 16

LEFT, ACROSS, CORE, CORE_ACROSS, RIGHT, RELAY, OUT = range(7)

ROUND = (2, 1, 3, 0)
VIA = ((2, 0), (1, 3))
def hops(offset):
    return sum(min(d, 4 - d) for d in offset)


STAGED = [(dx, dy) for dx in ROUND for dy in ROUND]
NEAR = sorted([(dx, dy) for dx in ROUND for dy in ROUND], key=hops, reverse=True)
DIRECT = [offset for offset in NEAR if hops(offset) <= 0]


LOAD_ORDER = (0, 7, 8, 9, 10, 3, 5, 1, 11, 12, 4, 6, 2, 15, 13, 14, 16)


def normalise(values):
    values = values.astype(F32)
    centre = jnp.mean(values, axis=-1, keepdims=True)
    shifted = values - centre
    spread = jnp.mean(shifted * shifted, axis=-1, keepdims=True)
    return shifted * lax.rsqrt(spread + EPSILON)


def sigmoid(values):
    return 0.5 * jnp.tanh(0.5 * values) + 0.5


def dot_nt(left, right):
    return lax.dot_general(left, right, (((1,), (1,)), ((), ())), preferred_element_type=F32)


def kernel(*refs):
    sources, refs = refs[:17], refs[17:]
    out, refs = refs[0], refs[1:]
    held, refs = refs[:17], refs[17:]
    (
        xl, xr, xt, row_flags, column_flags, key_scalars, key_rows,
        gain, bias, wlg, wlv, wrg, wrv, hgain, hbias, wog, wo,
    ) = held
    (
        nl, tl, tr, ls, lb, rs, rb, osc, av, ar, os_, cb, gate,
        sent, rl, rr, rz, rc, ra, ro, cs, loads,
    ) = refs
    pending = [
        pltpu.make_async_copy(src, dst, loads.at[n])
        for n, (src, dst) in enumerate(zip(sources, held))
    ]
    half = NI * NM // 2
    first_half, second_half = [
        pltpu.make_async_copy(
            sources[0].at[pl.ds(k * half, half)], xl.at[pl.ds(k * half, half)], loads.at[17 * k]
        )
        for k in range(2)
    ]
    first_half.start()
    for n in LOAD_ORDER[1:3]:
        pending[n].start()
    second_half.start()
    for n in LOAD_ORDER[3:]:
        pending[n].start()

    def loaded(*numbers):
        for n in numbers:
            pending[n].wait()

    row = lax.axis_index("row")
    col = lax.axis_index("col")
    depth = lax.axis_index("depth")
    x = lax.div(col, 4)
    low = lax.rem(col, 4)
    core_mate = x * 4 + low + 1 - 2 * lax.rem(low, 2)
    mate_low = lax.rem(low + 2, 4)
    z_mate = x * 4 + mate_low
    other_low = low + 1 - 2 * lax.rem(low, 2)

    def at(dx, dy, dz=0):
        return (
            lax.rem(row + dy, 4),
            lax.rem(x + dx, 4) * 4 + low,
            lax.rem(depth + dz, 4),
        )

    barrier = pltpu.get_barrier_semaphore()
    peers = [at(dx, dy, dz) for dz in (0, 1, 3) for dx, dy in NEAR if (dx, dy, dz) != (0, 0, 0)]
    peers.append((row, core_mate, depth))
    for offset in DIRECT:
        to_row, to_col, _ = at(*offset)
        peers.append((to_row, to_col - low + mate_low, depth))
    for peer in peers:
        pl.semaphore_signal(barrier, inc=1, device_id=peer, device_id_type=MESH)

    first_half.wait()
    loaded(7, 8)
    gains, biases = gain[...], bias[...]

    def left_norm(step, carry):
        rows = pl.ds(pl.multiple_of(step * 1024, 1024), 1024)
        nl[rows, :] = normalise(xl[rows, :]) * gains + biases
        return carry

    lax.fori_loop(0, NI * NM // 2048, left_norm, 0)
    second_half.wait()
    lax.fori_loop(NI * NM // 2048, NI * NM // 1024, left_norm, 0)
    loaded(9, 10, 3, 5)
    w_left = jnp.concatenate([wlg[...], wlv[...]], axis=1).astype(F32).T.astype(BF16)
    row_mask = row_flags[...].astype(F32)

    def left_act(step, carry):
        xs = jnp.concatenate(
            [nl[pl.ds(step * 8 + mm, NI, stride=NM), :] for mm in range(8)], axis=0
        ).astype(BF16)
        both = dot_nt(w_left, xs)
        act = sigmoid(both[:128]) * both[128:]
        for mm in range(8):
            key = key_scalars[depth, col * NM + step * 8 + mm].astype(F32)
            part = act[:, mm * NI : (mm + 1) * NI] * (row_mask * key)
            for d in range(16):
                tl[pl.ds(d * HB * NM + step * 8 + mm, HB, stride=NM), :] = part[d * HB : (d + 1) * HB]
        return carry

    lax.fori_loop(0, NM // 8, left_act, 0)

    pl.semaphore_wait(barrier, len(peers))

    def owner(dx, dy):
        return lax.rem(x + dx, 4) * 4 + lax.rem(row + dy, 4)

    def send(src, dst, kind, recv_sem, device):
        pltpu.make_async_remote_copy(
            src_ref=src, dst_ref=dst, send_sem=sent.at[kind], recv_sem=recv_sem,
            device_id=device, device_id_type=MESH,
        ).start()

    def received(dst, sem):
        pltpu.make_async_remote_copy(
            src_ref=dst, dst_ref=dst, send_sem=sem, recv_sem=sem,
            device_id=at(1, 0), device_id_type=MESH,
        ).wait_recv()

    def source(dx, dy):
        return lax.rem(x + 4 - dx, 4), lax.rem(row + 4 - dy, 4)

    for n, (dx, dy) in enumerate(NEAR):
        d = owner(dx, dy)
        rows = pl.ds(pl.multiple_of(d * HB * NM, HB * NM), HB * NM)
        ls[d] = tl[rows, :].astype(BF16).reshape(HB, NM, NI)
        target = lb.at[row, :, x, low]
        if (dx, dy) == (0, 0):
            pltpu.make_async_copy(ls.at[d], target, cs.at[0]).start()
            send(ls.at[d], target, CORE, rc.at[0], (row, core_mate, depth))
        else:
            send(ls.at[d], target, LEFT, rl.at[n], at(dx, dy))
        if (dx, dy) in DIRECT:
            to_row, to_col, _ = at(dx, dy)
            send(ls.at[d], target, ACROSS, rz.at[n], (to_row, to_col - low + mate_low, depth))

    loaded(1, 11, 12, 4, 6)
    w_right = jnp.concatenate([wrg[...], wrv[...]], axis=1).astype(F32).T.astype(BF16)
    key_block = key_rows[:, pl.ds(pl.multiple_of(row * NK, NK), NK)].astype(F32)
    here = lax.broadcasted_iota(jnp.int32, (4, NK), 0) == depth
    key_mask = jnp.sum(jnp.where(here, key_block, 0.0), axis=0, keepdims=True)

    def right_act(step, carry):
        rows = pl.ds(pl.multiple_of(step * 1664, 128), 1664)
        xs = (normalise(xr[rows, :]) * gains + biases).astype(BF16)
        both = dot_nt(w_right, xs)
        act = sigmoid(both[:128]) * both[128:]
        for jj in range(13):
            flag = column_flags[step * 13 + jj].astype(F32)
            part = act[:, jj * NK : (jj + 1) * NK] * (key_mask * flag)
            for d in range(16):
                tr[pl.ds(d * HB * NJ + step * 13 + jj, HB, stride=NJ), :] = part[d * HB : (d + 1) * HB]
        return carry

    lax.fori_loop(0, NJ // 13, right_act, 0)

    for n, (dx, dy) in enumerate(STAGED):
        d = owner(dx, dy)
        rows = pl.ds(pl.multiple_of(d * HB * NJ, HB * NJ), HB * NJ)
        if (dx, dy) == (0, 0):
            rb[x, row] = tr[rows, :].astype(BF16)
            continue
        rs[d] = tr[rows, :].astype(BF16)
        send(rs.at[d], rb.at[x, row], RIGHT, rr.at[ROUND.index(dx)], at(dx, dy))

    pltpu.make_async_copy(ls.at[owner(0, 0)], lb.at[row, :, x, low], cs.at[0]).wait()
    for n, offset in enumerate(NEAR):
        if offset == (0, 0):
            continue
        x_from, y_from = source(*offset)
        part = lb.at[y_from, :, x_from, low]
        received(part, rl.at[n])
        if offset not in DIRECT:
            send(part, part, ACROSS, rz.at[n], (row, z_mate, depth))
        send(part, part, CORE, rc.at[0], (row, core_mate, depth))

    for n, offset in [(15, (0, 0))] + list(enumerate(NEAR))[:15]:
        x_from, y_from = source(*offset)
        part = lb.at[y_from, :, x_from, mate_low]
        received(part, rz.at[n])
        send(part, part, CORE_ACROSS, rc.at[1], (row, core_mate, depth))
    mate_other = lax.rem(other_low + 2, 4)
    received(lb.at[:, :, :, other_low], rc.at[0])
    received(lb.at[:, :, :, mate_other], rc.at[1])

    osc[:, :, (BASE + NJ) * HB : (BASE + NJ + 1) * HB, :] = jnp.zeros((4, 4, HB, 128), F32)
    out_sends = []
    mine = x * 4 + row

    def block_of(stage, dy, dz):
        start = pl.multiple_of(BASE * HB + lax.rem(depth + dz, 4) * (NT * HB), HB)
        return osc[stage, lax.rem(row + dy, 4), pl.ds(start, MSG), :]

    def contract(stage, dx):
        x_from = lax.rem(x + 4 - dx, 4)
        received(rb.at[x_from] if dx else rb.at[x_from, pl.ds(0, 3)], rr.at[stage])
        for h in range(HB):
            first = h * NJ // 16 * 16
            skew = h * NJ - first
            lhs = jnp.concatenate([rb[x_from, y, first : first + 64, :] for y in range(4)], axis=1)
            for half in range(2):
                rhs = jnp.concatenate(
                    [lb[half * 2 + q, h].reshape(512, NI) for q in range(2)], axis=1
                )
                sums = jnp.dot(lhs, rhs, preferred_element_type=F32)
                for q in range(2):
                    osc[stage, half * 2 + q, pl.ds((BASE - skew) * HB + h, 64, stride=HB), :] = sums[
                        :, q * NI : (q + 1) * NI
                    ]
        for side, dz in enumerate((1, 3)):
            for k, dy in enumerate(VIA[side]):
                av[stage, side, k] = block_of(stage, dy, 2).astype(BF16)
            send(av.at[stage, side], ar.at[stage, side], RELAY, ra.at[stage], at(0, 0, dz))

    def distribute(stage, dx):
        x_from = lax.rem(x + 4 - dx, 4)
        received(ar.at[stage], ra.at[stage])
        for slot, dz in enumerate((1, 3, 0)):
            for dy in ROUND:
                block = block_of(stage, dy, dz)
                if slot < 2 and dy in VIA[slot]:
                    block = block + ar[stage, slot, VIA[slot].index(dy)].astype(F32)
                if (dx, dy, dz) == (0, 0, 0):
                    cb[slot * 16 + mine] = block.astype(BF16)
                    continue
                to_row, to_depth = lax.rem(row + dy, 4), lax.rem(depth + dz, 4)
                n = len(out_sends)
                os_[n] = block.astype(BF16)
                target = (to_row, x_from * 4 + low, to_depth)
                send(os_.at[n], cb.at[slot * 16 + mine], OUT, ro.at[0], target)
                out_sends.append((dx, dy, slot))

    for stage, dx in enumerate(ROUND):
        contract(stage, dx)
        if stage:
            distribute(stage - 1, ROUND[stage - 1])
    distribute(3, ROUND[3])

    loaded(2, 15, 13, 14, 16)
    tile_weight = wog[...]

    def tile_gate(j, carry):
        normed = (normalise(xt[j]) * gains + biases).astype(BF16)
        gate[j] = sigmoid(jnp.dot(normed, tile_weight, preferred_element_type=F32))
        return carry

    lax.fori_loop(0, NT, tile_gate, 0)

    received(cb.at[pl.ds(0, 47)], ro.at[0])

    hg = jnp.broadcast_to(hgain[...], (128, 128)).T
    hb = jnp.broadcast_to(hbias[...], (128, 128)).T
    weight = wo[...]

    def finish(j, sums):
        centre = jnp.mean(sums, axis=0, keepdims=True)
        shifted = sums - centre
        spread = jnp.mean(shifted * shifted, axis=0, keepdims=True)
        hidden = (shifted * lax.rsqrt(spread + EPSILON) * hg + hb).astype(BF16)
        projected = lax.dot_general(
            hidden, weight, (((0,), (0,)), ((), ())), preferred_element_type=F32
        )
        out[j] = (gate[j] * projected).astype(BF16)

    for p in range(JPAD // 2):
        rows = slice(p * 16, p * 16 + 16)
        total = cb[0:16, rows, :].astype(F32)
        for z in range(1, 3):
            total = total + cb[z * 16 : z * 16 + 16, rows, :].astype(F32)
        finish(p * 2, total[:, :HB].reshape(128, NI))
        if p < JPAD // 2 - 1:
            finish(p * 2 + 1, total[:, HB:].reshape(128, NI))

    for kind, part in (
        (LEFT, ls.at[pl.ds(0, 15)]), (ACROSS, ls), (CORE, ls), (CORE_ACROSS, ls),
        (RIGHT, rs.at[pl.ds(0, 15)]), (RELAY, av), (OUT, os_),
    ):
        pltpu.make_async_remote_copy(
            src_ref=part, dst_ref=part, send_sem=sent.at[kind], recv_sem=sent.at[kind],
            device_id=at(1, 0), device_id_type=MESH,
        ).wait_send()


def per_device(
    left_pair, right_pair, pair_tile, row_flags, column_flags, key_flags,
    input_gain, input_bias, left_gate_weight, left_value_weight,
    right_gate_weight, right_value_weight, hidden_gain, hidden_bias,
    output_gate_weight, output_weight,
):
    dma = pltpu.SemaphoreType.DMA
    operands = (
        left_pair.reshape(NI * NM, 128),
        right_pair.reshape(NJ * NK, 128),
        pair_tile.transpose(1, 0, 2),
        row_flags.reshape(1, NI),
        column_flags,
        key_flags,
        key_flags,
        input_gain.reshape(1, 128),
        input_bias.reshape(1, 128),
        left_gate_weight, left_value_weight, right_gate_weight, right_value_weight,
        hidden_gain.reshape(1, 128),
        hidden_bias.reshape(1, 128),
        output_gate_weight, output_weight,
    )
    held = [
        pltpu.SMEM(a.shape, a.dtype) if n in (4, 5) else pltpu.VMEM(a.shape, a.dtype)
        for n, a in enumerate(operands)
    ]
    result = pl.pallas_call(
        kernel,
        out_shape=jax.ShapeDtypeStruct((NT, NI, 128), BF16),
        in_specs=[pl.BlockSpec(memory_space=pltpu.HBM)] * len(operands),
        out_specs=pl.BlockSpec(memory_space=pltpu.VMEM),
        scratch_shapes=held + [
            pltpu.VMEM((NI * NM, 128), F32),
            pltpu.VMEM((16 * HB * NM, 128), F32),
            pltpu.VMEM((16 * HB * NJ, 128), F32),
            pltpu.VMEM((16, HB, NM, NI), BF16),
            pltpu.VMEM((4, HB, 4, 4, NM, NI), BF16),
            pltpu.VMEM((16, HB * NJ, NK), BF16),
            pltpu.VMEM((4, 4, HB * NJ, NK), BF16),
            pltpu.VMEM((4, 4, SLOTS * HB, 128), F32),
            pltpu.VMEM((4, 2, 2, MSG, 128), BF16),
            pltpu.VMEM((4, 2, 2, MSG, 128), BF16),
            pltpu.VMEM((47, MSG, 128), BF16),
            pltpu.VMEM((48, MSG, 128), BF16),
            pltpu.VMEM((NT, NI, 128), F32),
            dma((7,)), dma((15,)), dma((4,)), dma((16,)), dma((2,)), dma((4,)),
            dma((1,)), dma((1,)), dma((18,)),
        ],
        compiler_params=pltpu.CompilerParams(
            collective_id=0, has_side_effects=True, vmem_limit_bytes=60 * 2**20
        ),
        name="triangle",
    )(*operands)
    return result.transpose(1, 0, 2)


def solution(mesh):
    in_specs = (
        P("row", "depth", "col", None),
        P("col", "depth", "row", None),
        P("row", ("col", "depth"), None),
        P("row"),
        P("col"),
    ) + (P(),) * 11
    return jax.shard_map(
        per_device,
        mesh=mesh,
        in_specs=in_specs,
        out_specs=P("row", ("col", "depth"), None),
        check_vma=False,
    )
```
